128 devices in a mesh: img: 8 (over y, core), pair: 16 (over z, x).
Axes of the slice: x: 4, y: 4, z: 4, core: 2. Of those that a mesh axis runs over, the one named last changes fastest.
Arguments:
- encoder_tokens: bfloat16 [4096, 16, 1024], P(('img', 'pair')), may hold values from -6 to 6
- pair_owner: int32 [4096, 2], P(('img', 'pair')), may hold values from 0 to 127, as said below
- pair_local: int32 [4096, 2], P(('img', 'pair')), may hold values from 0 to 31
- w_embed: bfloat16 [1024, 768], replicated, may hold values from -0.1875 to 0.1875
- gain_query: float32 [768], replicated, may hold values from 0.5 to 14
- gain_key: float32 [768], replicated, may hold values from 0.5 to 14
- gain_out: float32 [768], replicated, may hold values from 0.25 to 1.75
- w_query: bfloat16 [768, 768], replicated, may hold values from -0.21875 to 0.21875
- w_key: bfloat16 [768, 768], replicated, may hold values from -0.21875 to 0.21875
- w_value: bfloat16 [768, 768], replicated, may hold values from -0.21875 to 0.21875
- w_out: bfloat16 [768, 768], replicated, may hold values from -0.21875 to 0.21875
- w_head: bfloat16 [768, 1024], replicated, may hold values from -0.21875 to 0.21875
Outputs:
- image_sums: bfloat16 [4096, 16, 1024], P(('img', 'pair'))
The draws below stay inside these ranges and needn't reach their ends.
Inputs may be any that keep to these rules, and one draw needn't show every extreme that they name: `pair_owner`: within the 32 rows of one device, the 64 entries are all different; one block value appears in every device's rows.
All inputs are finite; a program needn't handle non-finite values.
Results may differ from the reference program's by a relative error of at most 0.02.
The reference program's roundings to bfloat16 on the way count: a program that leaves them out, or rounds other values in their place, can miss the bound.
Values may be sent and summed in bfloat16 or wider, within the bound.
No kernel may reach another device: no remote copies, remote signals or barrier semaphores. Data moves between devices by JAX's collectives and lax.ppermute only.
A program may use at most 128 MiB of HBM per device.

```python
import jax
import jax.numpy as jnp
from jax import lax

ENC = 1024
DEC = 768
HEADS = 12
HD = 64
HEADOUT = 1024
TOK = 16
IMG_DEV = 32
PAIRS_DEV = 32
IMAGES = 4096
PAIRS = 4096


def draw_pair_owner(key, part):
    key = jax.random.fold_in(key, 11)
    devices = PAIRS // PAIRS_DEV
    width = 2 * PAIRS_DEV
    centre_key, rest_key = jax.random.split(key)
    centre = jax.random.randint(centre_key, (), 0, devices)
    keys = jax.random.split(rest_key, devices)

    def one_device(device_key):
        first_key, second_key = jax.random.split(device_key)
        others = jax.random.permutation(first_key, devices - 1)[:width - 1] + 1
        picks = jnp.concatenate([jnp.zeros((1,), jnp.int32), others.astype(jnp.int32)])
        order = jax.random.permutation(second_key, width)
        return (picks[order] + centre) % devices
    table = jax.vmap(one_device)(keys)
    return table.reshape(PAIRS, 2).astype(jnp.int32)


def draw_gain_query(key, part):
    key = jax.random.fold_in(key, 23)
    return jax.random.uniform(key, (DEC,), jnp.float32, 0.5, 2.0)


def draw_gain_key(key, part):
    key = jax.random.fold_in(key, 29)
    return jax.random.uniform(key, (DEC,), jnp.float32, 0.5, 2.0)


def set_ends(values, own_key, low, high):
    longest = values.shape.index(max(values.shape))
    spots = []
    for shift in (0, 1):
        where = [jax.random.randint(jax.random.fold_in(own_key, axis), (), 0, length) for axis, length in enumerate(values.shape)]
        where[longest] = (where[longest] + shift) % values.shape[longest]
        spots.append(tuple(where))
    return values.at[spots[0]].set(low).at[spots[1]].set(high)


def shard_levels(own_key, extent, cuts, smallest, largest):
    def one(position, shards_of):
        draws = jax.random.uniform(jax.random.fold_in(jax.random.fold_in(own_key, 6), position), (shards_of,), jnp.float32, smallest / len(cuts), largest / len(cuts))
        return jnp.repeat(jnp.exp(draws), extent[position] // shards_of).reshape((-1,) + (1,) * (len(extent) - position - 1))

    factor_of = one(*cuts[0])
    for cut in cuts[1:]:
        factor_of = factor_of * one(*cut)
    return factor_of


def normal_values(own_key, shape, scale, most, cuts=(), dtype=jnp.bfloat16):
    array = jax.random.normal(own_key, shape, jnp.float32) * scale
    if len(cuts) > 0:
        array = shard_levels(own_key, shape, cuts, -0.22, 0.18) * array
    return jnp.clip(array, min=-most, max=most).astype(dtype)


def setup_inputs(seed: int = 0) -> dict:
    streams_of = jax.random.split(jax.random.key(seed), 13)
    encoder_tokens = normal_values(streams_of[0], (IMAGES, TOK, ENC), 1.0, 6.0, ((0, 128),))
    pair_owner = draw_pair_owner(jax.random.fold_in(streams_of[12], 71), 0)
    pair_local = set_ends(jax.random.randint(streams_of[2], (PAIRS, 2), 0, IMG_DEV), jax.random.fold_in(streams_of[2], 1), 0, IMG_DEV - 1).astype(jnp.int32)
    w_embed = normal_values(streams_of[3], (ENC, DEC), ENC ** -0.5, 0.1875)
    gain_query = draw_gain_query(jax.random.fold_in(streams_of[12], 71), 0)
    gain_key = draw_gain_key(jax.random.fold_in(streams_of[12], 71), 0)
    gain_out = jnp.clip(1.0 + 0.15 * jax.random.normal(streams_of[6], (DEC,), jnp.float32), 0.25, 1.75)
    w_query = normal_values(streams_of[7], (DEC, DEC), DEC ** -0.5, 0.21875)
    w_key = normal_values(streams_of[8], (DEC, DEC), DEC ** -0.5, 0.21875)
    w_value = normal_values(streams_of[9], (DEC, DEC), DEC ** -0.5, 0.21875)
    w_out = normal_values(streams_of[10], (DEC, DEC), DEC ** -0.5, 0.21875)
    w_head = normal_values(streams_of[11], (DEC, HEADOUT), DEC ** -0.5, 0.21875)
    return dict(encoder_tokens=encoder_tokens, pair_owner=pair_owner, pair_local=pair_local, w_embed=w_embed, gain_query=gain_query, gain_key=gain_key, gain_out=gain_out, w_query=w_query, w_key=w_key, w_value=w_value, w_out=w_out, w_head=w_head)


def normed(values, gain):
    mean = lax.optimization_barrier(jnp.mean(values, axis=-1, keepdims=True))
    centred = values - mean
    spread = lax.optimization_barrier(jnp.mean(centred * centred, axis=-1, keepdims=True))
    return centred * lax.rsqrt(spread + 1e-05) * gain

def cross_decode(ends, context, weights_all):
    gain_query, gain_key, gain_out, w_query, w_key, w_value, w_out, w_head = weights_all
    count = ends.shape[0]
    tokens = ends.shape[2]
    width = ends.shape[3]
    query_in = normed(ends.astype(jnp.float32), gain_query).astype(jnp.bfloat16).astype(jnp.float32)
    context_in = normed(context.astype(jnp.float32), gain_key).astype(jnp.bfloat16).astype(jnp.float32)
    query = jnp.dot(query_in.reshape(-1, width), w_query).astype(jnp.bfloat16).astype(jnp.float32)
    key = jnp.dot(context_in.reshape(-1, width), w_key).astype(jnp.bfloat16).astype(jnp.float32)
    value = jnp.dot(context_in.reshape(-1, width), w_value).astype(jnp.bfloat16).astype(jnp.float32)
    shape = (count, 2, tokens, HEADS, HD)
    query = query.reshape(shape)
    key = key.reshape(shape)
    value = value.reshape(shape)
    scores = jnp.einsum('psqhd,pskhd->pshqk', query, key) * HD ** (-0.5)
    weights = jax.nn.softmax(scores, axis=-1).astype(jnp.bfloat16).astype(jnp.float32)
    attended = jnp.einsum('pshqk,pskhd->psqhd', weights, value).astype(jnp.bfloat16).astype(jnp.float32)
    hidden = ends.reshape(-1, width).astype(jnp.float32) + jnp.dot(attended.reshape(-1, width), w_out)
    head_in = normed(hidden, gain_out).astype(jnp.bfloat16).astype(jnp.float32)
    return jnp.dot(head_in, w_head).astype(jnp.bfloat16)

def reference(encoder_tokens, pair_owner, pair_local, w_embed, gain_query, gain_key, gain_out, w_query, w_key, w_value, w_out, w_head):
    images = encoder_tokens.shape[0]
    tokens = encoder_tokens.shape[1]
    embedded = jnp.dot(encoder_tokens.reshape(-1, ENC).astype(jnp.float32), w_embed.astype(jnp.float32))
    embedded = embedded.astype(jnp.bfloat16).reshape(images, tokens, DEC)
    weights_all = (gain_query, gain_key, gain_out, w_query.astype(jnp.float32), w_key.astype(jnp.float32), w_value.astype(jnp.float32), w_out.astype(jnp.float32), w_head.astype(jnp.float32))
    image_id = (pair_owner * IMG_DEV + pair_local).astype(jnp.int32)
    blocks = image_id.reshape(-1, PAIRS_DEV, 2)

    def one_block(totals, block_ids):
        ends = embedded[block_ids]
        context = ends[:, ::-1]
        result = cross_decode(ends, context, weights_all)
        result = result.reshape(-1, tokens, HEADOUT).astype(jnp.float32)
        return (totals.at[block_ids.reshape(-1)].add(result), None)
    totals = jnp.zeros((images, tokens, HEADOUT), jnp.float32)
    totals, unused = lax.scan(one_block, totals, blocks)
    return totals.astype(jnp.bfloat16)
```

```python
import functools

import jax
import jax.numpy as jnp
from jax import lax
from jax.experimental import pallas as pl
from jax.experimental.pallas import tpu as pltpu
from jax.sharding import PartitionSpec as P

HEADS = 12
HD = 64
TOK = 16
AXES = ("img", "pair")
GROUP = 8
BF16 = jnp.bfloat16
F32 = jnp.float32
MIB = 1024 * 1024


def exchange(blocks):
    return lax.all_to_all(blocks, AXES, split_axis=0, concat_axis=0, tiled=True)


def dot(a, b, contract):
    return lax.dot_general(a, b, (contract, ((), ())), preferred_element_type=F32)


def normalised(values):
    mean = jnp.mean(values, axis=-1, keepdims=True)
    centred = values - mean
    spread = jnp.mean(centred * centred, axis=-1, keepdims=True)
    return centred * lax.rsqrt(spread + 1e-05)


def fetch_kernel(asked, table, out, sem):
    devices = out.shape[0]
    owned = table.shape[0]

    def send(d, carry):
        image = jnp.clip(asked[d], 0, owned - 1)
        pltpu.make_async_copy(table.at[image], out.at[d], sem).start()
        return carry

    lax.fori_loop(0, devices, send, 0, unroll=8)
    pltpu.make_async_copy(out, out, sem).wait()


def fetch(asked, table, devices):
    return pl.pallas_call(
        fetch_kernel,
        out_shape=jax.ShapeDtypeStruct((devices,) + table.shape[1:], table.dtype),
        in_specs=[
            pl.BlockSpec(memory_space=pltpu.SMEM),
            pl.BlockSpec(memory_space=pltpu.VMEM),
        ],
        out_specs=pl.BlockSpec(memory_space=pl.ANY),
        scratch_shapes=[pltpu.SemaphoreType.DMA],
        name="fetch",
    )(asked, table)


def decode_kernel(
    owners,
    incoming,
    gain_query,
    gain_key,
    gain_out,
    w_query,
    w_key,
    w_value_t,
    w_out,
    out,
    ends,
    result,
    attended_t,
    in_sem,
    out_sem,
):
    images = ends.shape[0]
    width = ends.shape[2]
    step = 16
    rows = step * TOK
    block = GROUP * TOK

    def bring(i, carry):
        pltpu.make_async_copy(incoming.at[owners[i]], ends.at[i], in_sem).start()
        return carry

    lax.fori_loop(0, images, bring, 0, unroll=8)
    pltpu.make_async_copy(ends, ends, in_sem).wait()

    lane_image = lax.broadcasted_iota(jnp.int32, (TOK, block), 1) // TOK
    row_image = lax.broadcasted_iota(jnp.int32, (block, block), 0) // TOK
    column_image = lax.broadcasted_iota(jnp.int32, (block, block), 1) // TOK
    partner = ((row_image ^ 1) == column_image).astype(F32).astype(BF16)
    lane_head = lax.broadcasted_iota(jnp.int32, (block, 2 * HD), 1) // HD
    head_mask = [(lane_head == h).astype(F32).astype(BF16) for h in range(2)]

    def one(it, carry):
        x = ends[pl.ds(it * step, step)].reshape(rows, width).astype(F32)
        xn = normalised(x)
        query_in = (xn * gain_query[...]).astype(BF16)
        context_in = (xn * gain_key[...]).astype(BF16)
        query = dot(query_in, w_query[...], ((1,), (0,))).astype(BF16)
        key = dot(context_in, w_key[...], ((1,), (0,))).astype(BF16)
        value_t = dot(w_value_t[...], context_in, ((1,), (1,))).astype(BF16)
        for g in range(rows // block):
            at = slice(g * block, (g + 1) * block)
            for pair in range(HEADS // 2):
                lanes = slice(pair * 2 * HD, (pair + 1) * 2 * HD)
                q = query[at, lanes]
                k = key[at, lanes]
                for h in range(2):
                    s_t = dot(k * head_mask[h], q, ((1,), (1,)))
                    parts = [s_t[j * TOK:(j + 1) * TOK] for j in range(GROUP)]
                    scores = parts[1]
                    for i in range(1, GROUP):
                        scores = jnp.where(lane_image == i, parts[i ^ 1], scores)
                    scores = scores * (HD ** -0.5)
                    top = jnp.max(scores, axis=0, keepdims=True)
                    e = jnp.exp(scores - top)
                    weights = (e / jnp.sum(e, axis=0, keepdims=True)).astype(BF16)
                    p_t = jnp.concatenate([weights] * GROUP, axis=0) * partner
                    head = 2 * pair + h
                    v_t = value_t[head * HD:(head + 1) * HD, at]
                    attended_t[head * HD:(head + 1) * HD, at] = dot(
                        v_t, p_t, ((1,), (0,))
                    ).astype(BF16)
        hidden = x + dot(attended_t[...], w_out[...], ((0,), (0,)))
        head_in = (normalised(hidden) * gain_out[...]).astype(BF16)
        result[pl.ds(it * step, step)] = head_in.reshape(step, TOK, width)

        def give(i, carry):
            i = it * step + i
            pltpu.make_async_copy(result.at[i], out.at[owners[i]], out_sem).start()
            return carry

        lax.fori_loop(0, step, give, 0, unroll=8)
        return carry

    lax.fori_loop(0, images // step, one, 0)
    pltpu.make_async_copy(result, result, out_sem).wait()


def decode(owners, incoming, gain_query, gain_key, gain_out, w_query, w_key, w_value_t, w_out):
    images = owners.shape[0]
    devices, tokens, width = incoming.shape
    vmem = pl.BlockSpec(memory_space=pltpu.VMEM)
    rows = 16 * tokens
    return pl.pallas_call(
        decode_kernel,
        out_shape=jax.ShapeDtypeStruct(incoming.shape, BF16),
        in_specs=[
            pl.BlockSpec(memory_space=pltpu.SMEM),
            pl.BlockSpec(memory_space=pl.ANY),
        ] + [vmem] * 7,
        out_specs=pl.BlockSpec(memory_space=pl.ANY),
        scratch_shapes=[
            pltpu.VMEM((images, tokens, width), BF16),
            pltpu.VMEM((images, tokens, width), BF16),
            pltpu.VMEM((width, rows), BF16),
            pltpu.SemaphoreType.DMA,
            pltpu.SemaphoreType.DMA,
        ],
        compiler_params=pltpu.CompilerParams(vmem_limit_bytes=40 * MIB),
        name="decode",
    )(owners, incoming, gain_query, gain_key, gain_out, w_query, w_key, w_value_t, w_out)


def total_kernel(asked, returned, w_head, out, arrived, sums, sem):
    devices, tokens, width = arrived.shape
    owned = out.shape[0]
    copy = pltpu.make_async_copy(returned, arrived, sem)
    copy.start()
    sums[...] = jnp.zeros_like(sums)
    copy.wait()

    def add(d, carry):
        image = jnp.where(asked[d] >= 0, asked[d], owned)
        sums[image] += arrived[d].astype(F32)
        return carry

    lax.fori_loop(0, devices, add, 0, unroll=4)
    total = sums[:owned].reshape(owned * tokens, width)
    upper = total.astype(BF16)
    lower = (total - upper.astype(F32)).astype(BF16)
    head = dot(upper, w_head[...], ((1,), (0,))) + dot(lower, w_head[...], ((1,), (0,)))
    out[...] = head.astype(BF16).reshape(out.shape)


def total(asked, returned, w_head, owned):
    devices, tokens, width = returned.shape
    return pl.pallas_call(
        total_kernel,
        out_shape=jax.ShapeDtypeStruct((owned, tokens, w_head.shape[1]), BF16),
        in_specs=[
            pl.BlockSpec(memory_space=pltpu.SMEM),
            pl.BlockSpec(memory_space=pl.ANY),
            pl.BlockSpec(memory_space=pltpu.VMEM),
        ],
        out_specs=pl.BlockSpec(memory_space=pltpu.VMEM),
        scratch_shapes=[
            pltpu.VMEM(returned.shape, BF16),
            pltpu.VMEM((owned + 1, tokens, width), F32),
            pltpu.SemaphoreType.DMA,
        ],
        compiler_params=pltpu.CompilerParams(vmem_limit_bytes=40 * MIB),
        name="total",
    )(asked, returned, w_head)


def on_device(
    encoder_tokens,
    pair_owner,
    pair_local,
    w_embed,
    gain_query,
    gain_key,
    gain_out,
    w_query,
    w_key,
    w_value,
    w_out,
    w_head,
):
    devices = lax.axis_size(AXES)
    owned, tokens, _ = encoder_tokens.shape
    owners = pair_owner.reshape(-1)
    local = pair_local.reshape(-1)
    matches = owners[:, None] == jnp.arange(devices, dtype=jnp.int32)[None, :]
    wanted = jnp.sum(jnp.where(matches, local[:, None] + 1, 0), axis=0) - 1
    asked = exchange(wanted[:, None])[:, 0]
    table = jnp.dot(
        encoder_tokens.reshape(owned * tokens, -1), w_embed, preferred_element_type=F32
    ).astype(BF16).reshape(owned, tokens, -1)
    incoming = exchange(fetch(asked, table, devices))
    going_back = decode(
        owners,
        incoming,
        gain_query[None],
        gain_key[None],
        gain_out[None],
        w_query,
        w_key,
        w_value.T,
        w_out,
    )
    return total(asked, exchange(going_back), w_head, owned)


def solution(mesh):
    spec = P(AXES)
    return jax.shard_map(
        on_device,
        mesh=mesh,
        in_specs=(spec,) * 3 + (P(),) * 9,
        out_specs=spec,
        check_vma=False,
    )
```

```python
import jax
import jax.numpy as jnp
from jax import lax
from jax.experimental import pallas as pl
from jax.experimental.pallas import tpu as pltpu
from jax.sharding import PartitionSpec as P

HEADS = 12
HD = 64
TOK = 16
AXES = ("img", "pair")
GROUP = 8
QUAD = 4
STEP = 32
BF16 = jnp.bfloat16
F32 = jnp.float32
MIB = 1024 * 1024
VMEM = pl.BlockSpec(memory_space=pltpu.VMEM)
SMEM = pl.BlockSpec(memory_space=pltpu.SMEM)
HBM = pl.BlockSpec(memory_space=pltpu.HBM)


def exchange(blocks):
    return lax.all_to_all(blocks, AXES, split_axis=0, concat_axis=0, tiled=True)


def dot(a, b, contract):
    return lax.dot_general(a, b, (contract, ((), ())), preferred_element_type=F32)


def normalised(values):
    mean = jnp.mean(values, axis=-1, keepdims=True)
    centred = values - mean
    spread = jnp.mean(centred * centred, axis=-1, keepdims=True)
    return centred * lax.rsqrt(spread + 1e-05)


def ask_kernel(owner_hbm, local_hbm, out, owner, local, sem):
    devices = out.shape[0]
    sides, slots = owner.shape
    copies = [
        pltpu.make_async_copy(owner_hbm, owner, sem.at[0]),
        pltpu.make_async_copy(local_hbm, local, sem.at[1]),
    ]
    for copy in copies:
        copy.start()
    for copy in copies:
        copy.wait()
    device = lax.broadcasted_iota(jnp.int32, (devices, slots), 0)
    found = jnp.zeros((devices, slots), jnp.int32)
    for side in range(sides):
        match = device == owner[side:side + 1, :]
        found = jnp.where(match, local[side:side + 1, :] + 1, found)
    wanted = jnp.sum(found, axis=1, keepdims=True) - 1
    out[...] = jnp.broadcast_to(wanted, out.shape)


def ask(owner, local, devices):
    return pl.pallas_call(
        ask_kernel,
        out_shape=jax.ShapeDtypeStruct((devices, devices), jnp.int32),
        in_specs=[HBM, HBM],
        out_specs=VMEM,
        scratch_shapes=[
            pltpu.VMEM(owner.shape, jnp.int32),
            pltpu.VMEM(owner.shape, jnp.int32),
            pltpu.SemaphoreType.DMA((2,)),
        ],
        compiler_params=pltpu.CompilerParams(vmem_limit_bytes=62 * MIB),
        name="ask",
    )(owner, local)


def fetch_kernel(rows, table, out, asked, scalars, sem, block_sem):
    devices = out.shape[0]
    owned = table.shape[0]
    square = rows.shape
    across = lax.broadcasted_iota(jnp.int32, square, 0) == lax.broadcasted_iota(jnp.int32, square, 1)
    asked[...] = jnp.sum(jnp.where(across, rows[...], 0), axis=0, keepdims=True)
    copy = pltpu.make_async_copy(asked, scalars, sem)
    copy.start()
    copy.wait()

    def send(d, carry):
        image = jnp.clip(scalars[0, d], 0, owned - 1)
        pltpu.make_async_copy(table.at[image], out.at[d], block_sem).start()
        return carry

    lax.fori_loop(0, devices, send, 0, unroll=8)
    pltpu.make_async_copy(out, out, block_sem).wait()


def fetch(rows, table):
    devices = rows.shape[0]
    return pl.pallas_call(
        fetch_kernel,
        out_shape=[
            jax.ShapeDtypeStruct((devices,) + table.shape[1:], table.dtype),
            jax.ShapeDtypeStruct((1, devices), jnp.int32),
        ],
        in_specs=[VMEM, VMEM],
        out_specs=[HBM, VMEM],
        scratch_shapes=[
            pltpu.SMEM((1, devices), jnp.int32),
            pltpu.SemaphoreType.DMA,
            pltpu.SemaphoreType.DMA,
        ],
        compiler_params=pltpu.CompilerParams(vmem_limit_bytes=61 * MIB),
        name="fetch",
    )(rows, table)


def decode_kernel(
    owner,
    incoming,
    gain_query,
    gain_key,
    gain_out,
    w_query_hbm,
    w_key_hbm,
    w_value_t_hbm,
    w_out_hbm,
    out,
    ends,
    result,
    attended_t,
    w_query,
    w_key,
    w_value_t,
    w_out,
    in_sem,
    weight_sem,
    out_sem,
):
    images, _, width = ends.shape
    rows = STEP * TOK
    block = GROUP * TOK

    loads = [
        pltpu.make_async_copy(w_query_hbm, w_query, weight_sem.at[0]),
        pltpu.make_async_copy(w_key_hbm, w_key, weight_sem.at[1]),
        pltpu.make_async_copy(w_value_t_hbm, w_value_t, weight_sem.at[2]),
        pltpu.make_async_copy(w_out_hbm, w_out, weight_sem.at[3]),
    ]

    def bring(it):
        for i in range(it * STEP, (it + 1) * STEP):
            device = owner[i % 2, i // 2]
            pltpu.make_async_copy(incoming.at[device], ends.at[i], in_sem.at[it]).start()

    bring(0)
    for load in loads:
        load.start()
    for it in range(1, images // STEP):
        bring(it)

    lane_image = lax.broadcasted_iota(jnp.int32, (TOK, block), 1) // TOK
    row_image = lax.broadcasted_iota(jnp.int32, (block, block), 0) // TOK
    column_image = lax.broadcasted_iota(jnp.int32, (block, block), 1) // TOK
    partner = ((row_image ^ 1) == column_image).astype(F32).astype(BF16)
    lane_head = lax.broadcasted_iota(jnp.int32, (block, QUAD * HD), 1) // HD
    head_mask = [(lane_head == h).astype(F32).astype(BF16) for h in range(QUAD)]
    to_query = gain_query[...].reshape(1, width)
    to_key = gain_key[...].reshape(1, width)
    to_out = gain_out[...].reshape(1, width)

    for it in range(images // STEP):
        here = ends.at[it * STEP:(it + 1) * STEP]
        pltpu.make_async_copy(here, here, in_sem.at[it]).wait()
        x = ends[it * STEP:(it + 1) * STEP].reshape(rows, width).astype(F32)
        xn = normalised(x)
        query_in = (xn * to_query).astype(BF16)
        context_in = (xn * to_key).astype(BF16)
        if it == 0:
            loads[0].wait()
        query = dot(query_in, w_query[...], ((1,), (0,))).astype(BF16)
        if it == 0:
            loads[1].wait()
        key = dot(context_in, w_key[...], ((1,), (0,))).astype(BF16)
        if it == 0:
            loads[2].wait()
        value_t = dot(w_value_t[...], context_in, ((1,), (1,))).astype(BF16)
        for g in range(rows // block):
            at = slice(g * block, (g + 1) * block)
            compact = []
            for c in range(HEADS // QUAD):
                lanes = slice(c * QUAD * HD, (c + 1) * QUAD * HD)
                masked = [key[at, lanes] * head_mask[h] for h in range(QUAD)]
                s_t = dot(jnp.concatenate(masked, axis=0), query[at, lanes], ((1,), (1,)))
                s_t = s_t.reshape(QUAD, GROUP, TOK, block)
                for h in range(QUAD):
                    scores = s_t[h, 1]
                    for i in range(1, GROUP):
                        scores = jnp.where(lane_image == i, s_t[h, i ^ 1], scores)
                    compact.append(scores)
            scores = jnp.stack(compact) * (HD ** -0.5)
            e = jnp.exp(scores - jnp.max(scores, axis=1, keepdims=True))
            weights = (e / jnp.sum(e, axis=1, keepdims=True)).astype(BF16)
            for head in range(HEADS):
                p_t = jnp.concatenate([weights[head]] * GROUP, axis=0) * partner
                features = slice(head * HD, (head + 1) * HD)
                attended_t[features, at] = dot(
                    value_t[features, at], p_t, ((1,), (0,))
                ).astype(BF16)
        if it == 0:
            loads[3].wait()
        hidden = x + dot(attended_t[...], w_out[...], ((0,), (0,)))
        head_in = (normalised(hidden) * to_out).astype(BF16)
        result[it * STEP:(it + 1) * STEP] = head_in.reshape(STEP, TOK, width)
        for i in range(it * STEP, (it + 1) * STEP):
            device = owner[i % 2, i // 2]
            pltpu.make_async_copy(result.at[i], out.at[device], out_sem).start()
    pltpu.make_async_copy(result, result, out_sem).wait()


def decode(owner, incoming, gain_query, gain_key, gain_out, w_query, w_key, w_value_t, w_out):
    images = owner.size
    devices, tokens, width = incoming.shape
    return pl.pallas_call(
        decode_kernel,
        out_shape=jax.ShapeDtypeStruct(incoming.shape, BF16),
        in_specs=[SMEM, HBM] + [VMEM] * 3 + [HBM] * 4,
        out_specs=HBM,
        scratch_shapes=[
            pltpu.VMEM((images, tokens, width), BF16),
            pltpu.VMEM((images, tokens, width), BF16),
            pltpu.VMEM((width, STEP * tokens), BF16),
            pltpu.VMEM(w_query.shape, BF16),
            pltpu.VMEM(w_key.shape, BF16),
            pltpu.VMEM(w_value_t.shape, BF16),
            pltpu.VMEM(w_out.shape, BF16),
            pltpu.SemaphoreType.DMA((images // STEP,)),
            pltpu.SemaphoreType.DMA((4,)),
            pltpu.SemaphoreType.DMA,
        ],
        compiler_params=pltpu.CompilerParams(vmem_limit_bytes=62 * MIB),
        name="decode",
    )(owner, incoming, gain_query, gain_key, gain_out, w_query, w_key, w_value_t, w_out)


def total_kernel(asked, returned, w_head, out, sums):
    devices, tokens, width = returned.shape
    owned = out.shape[0]
    sums[...] = jnp.zeros_like(sums)

    def add(d, carry):
        image = jnp.where(asked[0, d] >= 0, asked[0, d], owned)
        sums[image] += returned[d].astype(F32)
        return carry

    lax.fori_loop(0, devices, add, 0, unroll=4)
    whole = sums[:owned].reshape(owned * tokens, width)
    upper = whole.astype(BF16)
    lower = (whole - upper.astype(F32)).astype(BF16)
    head = dot(upper, w_head[...], ((1,), (0,))) + dot(lower, w_head[...], ((1,), (0,)))
    out[...] = head.astype(BF16).reshape(out.shape)


def total(asked, returned, w_head, owned):
    devices, tokens, width = returned.shape
    return pl.pallas_call(
        total_kernel,
        out_shape=jax.ShapeDtypeStruct((owned, tokens, w_head.shape[1]), BF16),
        in_specs=[SMEM, VMEM, VMEM],
        out_specs=VMEM,
        scratch_shapes=[pltpu.VMEM((owned + 1, tokens, width), F32)],
        compiler_params=pltpu.CompilerParams(vmem_limit_bytes=24 * MIB),
        name="total",
    )(asked, returned, w_head)


def on_device(
    encoder_tokens,
    pair_owner,
    pair_local,
    w_embed,
    gain_query,
    gain_key,
    gain_out,
    w_query,
    w_key,
    w_value,
    w_out,
    w_head,
):
    devices = lax.axis_size(AXES)
    owned, tokens, _ = encoder_tokens.shape
    owner = pair_owner.T
    rows = exchange(ask(owner, pair_local.T, devices))
    table = jnp.dot(
        encoder_tokens.reshape(owned * tokens, -1), w_embed, preferred_element_type=F32
    ).astype(BF16).reshape(owned, tokens, -1)
    outgoing, asked = fetch(rows, table)
    incoming = exchange(outgoing)
    going_back = decode(
        owner, incoming, gain_query, gain_key, gain_out, w_query, w_key, w_value.T, w_out
    )
    return total(asked, exchange(going_back), w_head, owned)


def solution(mesh):
    spec = P(AXES)
    return jax.shard_map(
        on_device,
        mesh=mesh,
        in_specs=(spec,) * 3 + (P(),) * 9,
        out_specs=spec,
        check_vma=False,
    )
```

```python
import jax
import jax.numpy as jnp
from jax import lax
from jax.experimental import pallas as pl
from jax.experimental.pallas import tpu as pltpu
from jax.sharding import PartitionSpec as P

HEADS = 12
HD = 64
TOK = 16
AXES = ("img", "pair")
GROUP = 8
QUAD = 4
STEP = 32
BF16 = jnp.bfloat16
F32 = jnp.float32
MIB = 1024 * 1024
VMEM = pl.BlockSpec(memory_space=pltpu.VMEM)
SMEM = pl.BlockSpec(memory_space=pltpu.SMEM)
HBM = pl.BlockSpec(memory_space=pltpu.HBM)


def exchange(blocks):
    return lax.all_to_all(blocks, AXES, split_axis=0, concat_axis=0, tiled=True)


def dot(a, b, contract):
    return lax.dot_general(a, b, (contract, ((), ())), preferred_element_type=F32)


def normalised(values):
    mean = jnp.mean(values, axis=-1, keepdims=True)
    centred = values - mean
    spread = jnp.mean(centred * centred, axis=-1, keepdims=True)
    return centred * lax.rsqrt(spread + 1e-05)


def ask_kernel(owner_hbm, local_hbm, out, owner, local, sem):
    devices = out.shape[0]
    sides, slots = owner.shape
    copies = [
        pltpu.make_async_copy(owner_hbm, owner, sem.at[0]),
        pltpu.make_async_copy(local_hbm, local, sem.at[1]),
    ]
    for copy in copies:
        copy.start()
    for copy in copies:
        copy.wait()
    device = lax.broadcasted_iota(jnp.int32, (devices, slots), 0)
    found = jnp.zeros((devices, slots), jnp.int32)
    for side in range(sides):
        match = device == owner[side:side + 1, :]
        found = jnp.where(match, local[side:side + 1, :] + 1, found)
    wanted = jnp.sum(found, axis=1, keepdims=True) - 1
    out[...] = jnp.broadcast_to(wanted, out.shape)


def ask(owner, local, devices):
    return pl.pallas_call(
        ask_kernel,
        out_shape=jax.ShapeDtypeStruct((devices, devices), jnp.int32),
        in_specs=[HBM, HBM],
        out_specs=VMEM,
        scratch_shapes=[
            pltpu.VMEM(owner.shape, jnp.int32),
            pltpu.VMEM(owner.shape, jnp.int32),
            pltpu.SemaphoreType.DMA((2,)),
        ],
        compiler_params=pltpu.CompilerParams(vmem_limit_bytes=62 * MIB),
        name="ask",
    )(owner, local)


def fetch_kernel(rows, table, out, asked, scalars, sem):
    devices = out.shape[0]
    owned = table.shape[0]
    square = rows.shape
    across = lax.broadcasted_iota(jnp.int32, square, 0) == lax.broadcasted_iota(jnp.int32, square, 1)
    asked[...] = jnp.sum(jnp.where(across, rows[...], 0), axis=0, keepdims=True)
    copy = pltpu.make_async_copy(asked, scalars, sem)
    copy.start()
    copy.wait()
    for d in range(devices):
        out[d] = table[jnp.clip(scalars[0, d], 0, owned - 1)]


def fetch(rows, table):
    devices = rows.shape[0]
    return pl.pallas_call(
        fetch_kernel,
        out_shape=[
            jax.ShapeDtypeStruct((devices,) + table.shape[1:], table.dtype),
            jax.ShapeDtypeStruct((1, devices), jnp.int32),
        ],
        in_specs=[VMEM, VMEM],
        out_specs=[VMEM, VMEM],
        scratch_shapes=[pltpu.SMEM((1, devices), jnp.int32), pltpu.SemaphoreType.DMA],
        compiler_params=pltpu.CompilerParams(vmem_limit_bytes=16 * MIB),
        name="fetch",
    )(rows, table)


def decode_kernel(
    owner,
    incoming,
    gain_query,
    gain_key,
    gain_out,
    w_query,
    w_key,
    w_value,
    w_out,
    out,
    attended_t,
    w_value_t,
):
    images = owner.shape[0] * owner.shape[1]
    width = incoming.shape[2]
    rows = STEP * TOK
    block = GROUP * TOK

    lane_image = lax.broadcasted_iota(jnp.int32, (TOK, block), 1) // TOK
    row_image = lax.broadcasted_iota(jnp.int32, (block, block), 0) // TOK
    column_image = lax.broadcasted_iota(jnp.int32, (block, block), 1) // TOK
    partner = ((row_image ^ 1) == column_image).astype(F32).astype(BF16)
    lane_head = lax.broadcasted_iota(jnp.int32, (block, QUAD * HD), 1) // HD
    head_mask = [(lane_head == h).astype(F32).astype(BF16) for h in range(QUAD)]
    to_query = gain_query[...].reshape(1, width)
    to_key = gain_key[...].reshape(1, width)
    to_out = gain_out[...].reshape(1, width)

    for it in range(images // STEP):
        here = [owner[i % 2, i // 2] for i in range(it * STEP, (it + 1) * STEP)]
        x = jnp.stack([incoming[device] for device in here]).reshape(rows, width).astype(F32)
        xn = normalised(x)
        query_in = (xn * to_query).astype(BF16)
        context_in = (xn * to_key).astype(BF16)
        query = dot(query_in, w_query[...], ((1,), (0,))).astype(BF16)
        key = dot(context_in, w_key[...], ((1,), (0,))).astype(BF16)
        if it == 0:
            w_value_t[...] = w_value[...].T
        value_t = dot(w_value_t[...], context_in, ((1,), (1,))).astype(BF16)

        def score(g):
            at = slice(g * block, (g + 1) * block)
            compact = []
            for c in range(HEADS // QUAD):
                lanes = slice(c * QUAD * HD, (c + 1) * QUAD * HD)
                masked = [key[at, lanes] * head_mask[h] for h in range(QUAD)]
                s_t = dot(jnp.concatenate(masked, axis=0), query[at, lanes], ((1,), (1,)))
                s_t = s_t.reshape(QUAD, GROUP, TOK, block)
                for h in range(QUAD):
                    scores = s_t[h, 1]
                    for i in range(1, GROUP):
                        scores = jnp.where(lane_image == i, s_t[h, i ^ 1], scores)
                    compact.append(scores)
            return jnp.stack(compact) * (HD ** -0.5)

        def softmax(scores):
            e = jnp.exp(scores - jnp.max(scores, axis=1, keepdims=True))
            return (e / jnp.sum(e, axis=1, keepdims=True)).astype(BF16)

        def attend(g, weights):
            at = slice(g * block, (g + 1) * block)
            for head in range(HEADS):
                p_t = jnp.concatenate([weights[head]] * GROUP, axis=0) * partner
                features = slice(head * HD, (head + 1) * HD)
                attended_t[features, at] = dot(
                    value_t[features, at], p_t, ((1,), (0,))
                ).astype(BF16)

        groups = rows // block
        scores, weights = score(0), None
        for g in range(groups + 1):
            later = score(g + 1) if g + 1 < groups else None
            if weights is not None:
                attend(g - 1, weights)
            weights = softmax(scores) if scores is not None else None
            scores = later
        hidden = x + dot(attended_t[...], w_out[...], ((0,), (0,)))
        head_in = (normalised(hidden) * to_out).astype(BF16).reshape(STEP, TOK, width)
        for i in range(STEP):
            out[here[i]] = head_in[i]


def decode(owner, incoming, *parameters):
    images = owner.size
    devices, tokens, width = incoming.shape
    return pl.pallas_call(
        decode_kernel,
        out_shape=jax.ShapeDtypeStruct(incoming.shape, BF16),
        in_specs=[SMEM] + [VMEM] * 8,
        out_specs=VMEM,
        scratch_shapes=[
            pltpu.VMEM((width, STEP * tokens), BF16),
            pltpu.VMEM((width, width), BF16),
        ],
        compiler_params=pltpu.CompilerParams(vmem_limit_bytes=40 * MIB),
        name="decode",
    )(owner, incoming, *parameters)


def total_kernel(asked, returned, w_head, out, even, odd, result, sem):
    devices, tokens, width = returned.shape
    owned = out.shape[0]
    even[...] = jnp.zeros_like(even)
    odd[...] = jnp.zeros_like(odd)
    for d in range(devices):
        sums = odd if d % 2 else even
        image = jnp.where(asked[0, d] >= 0, asked[0, d], owned)
        sums[image] += returned[d].astype(F32)
    part = owned // sem.shape[0]
    copies = []
    for n in range(sem.shape[0]):
        at = slice(n * part, (n + 1) * part)
        whole = (even[at] + odd[at]).reshape(part * tokens, width).astype(BF16)
        head = dot(whole, w_head[...], ((1,), (0,))).astype(BF16)
        result[at] = head.reshape(part, tokens, w_head.shape[1])
        copies.append(pltpu.make_async_copy(result.at[at], out.at[at], sem.at[n]))
        copies[-1].start()
    for copy in copies:
        copy.wait()


def total(asked, returned, w_head, owned):
    devices, tokens, width = returned.shape
    shape = (owned, tokens, w_head.shape[1])
    return pl.pallas_call(
        total_kernel,
        out_shape=jax.ShapeDtypeStruct(shape, BF16),
        in_specs=[SMEM, VMEM, VMEM],
        out_specs=HBM,
        scratch_shapes=[
            pltpu.VMEM((owned + 1, tokens, width), F32),
            pltpu.VMEM((owned + 1, tokens, width), F32),
            pltpu.VMEM(shape, BF16),
            pltpu.SemaphoreType.DMA((2,)),
        ],
        compiler_params=pltpu.CompilerParams(vmem_limit_bytes=24 * MIB),
        name="total",
    )(asked, returned, w_head)


def on_device(
    encoder_tokens,
    pair_owner,
    pair_local,
    w_embed,
    gain_query,
    gain_key,
    gain_out,
    w_query,
    w_key,
    w_value,
    w_out,
    w_head,
):
    devices = lax.axis_size(AXES)
    owned, tokens, _ = encoder_tokens.shape
    owner = pair_owner.T
    rows = exchange(ask(owner, pair_local.T, devices))
    table = jnp.dot(
        encoder_tokens.reshape(owned * tokens, -1), w_embed, preferred_element_type=F32
    ).astype(BF16).reshape(owned, tokens, -1)
    outgoing, asked = fetch(rows, table)
    incoming = exchange(outgoing)
    going_back = decode(
        owner, incoming, gain_query, gain_key, gain_out, w_query, w_key, w_value, w_out
    )
    return total(asked, exchange(going_back), w_head, owned)


def solution(mesh):
    spec = P(AXES)
    return jax.shard_map(
        on_device,
        mesh=mesh,
        in_specs=(spec,) * 3 + (P(),) * 9,
        out_specs=spec,
        check_vma=False,
    )
```

```python
import jax
import jax.numpy as jnp
from jax import lax
from jax.experimental import pallas as pl
from jax.experimental.pallas import tpu as pltpu
from jax.sharding import PartitionSpec as P

HEADS = 12
HD = 64
TOK = 16
AXES = ("img", "pair")
GROUP = 8
QUAD = 4
STEP = 32
BF16 = jnp.bfloat16
F32 = jnp.float32
MIB = 1024 * 1024
VMEM = pl.BlockSpec(memory_space=pltpu.VMEM)
SMEM = pl.BlockSpec(memory_space=pltpu.SMEM)
HBM = pl.BlockSpec(memory_space=pltpu.HBM)


def exchange(blocks):
    return lax.all_to_all(blocks, AXES, split_axis=0, concat_axis=0, tiled=True)


def dot(a, b, contract):
    return lax.dot_general(a, b, (contract, ((), ())), preferred_element_type=F32)


def normalised(values):
    mean = jnp.mean(values, axis=-1, keepdims=True)
    centred = values - mean
    spread = jnp.mean(centred * centred, axis=-1, keepdims=True)
    return centred * lax.rsqrt(spread + 1e-05)


def ask_kernel(owner_hbm, local_hbm, out, owner, local, sem):
    devices = out.shape[0]
    sides, slots = owner.shape
    copies = [
        pltpu.make_async_copy(owner_hbm, owner, sem.at[0]),
        pltpu.make_async_copy(local_hbm, local, sem.at[1]),
    ]
    for copy in copies:
        copy.start()
    for copy in copies:
        copy.wait()
    device = lax.broadcasted_iota(jnp.int32, (devices, slots), 0)
    found = jnp.zeros((devices, slots), jnp.int32)
    for side in range(sides):
        match = device == owner[side:side + 1, :]
        found = jnp.where(match, local[side:side + 1, :] + 1, found)
    wanted = jnp.sum(found, axis=1, keepdims=True) - 1
    out[...] = jnp.broadcast_to(wanted, out.shape)


def ask(owner, local, devices):
    return pl.pallas_call(
        ask_kernel,
        out_shape=jax.ShapeDtypeStruct((devices, devices), jnp.int32),
        in_specs=[HBM, HBM],
        out_specs=VMEM,
        scratch_shapes=[
            pltpu.VMEM(owner.shape, jnp.int32),
            pltpu.VMEM(owner.shape, jnp.int32),
            pltpu.SemaphoreType.DMA((2,)),
        ],
        compiler_params=pltpu.CompilerParams(vmem_limit_bytes=62 * MIB),
        name="ask",
    )(owner, local)


def fetch_kernel(rows, table, out, asked, scalars, sem):
    devices = out.shape[0]
    owned = table.shape[0]
    square = rows.shape
    across = lax.broadcasted_iota(jnp.int32, square, 0) == lax.broadcasted_iota(jnp.int32, square, 1)
    asked[...] = jnp.sum(jnp.where(across, rows[...], 0), axis=0, keepdims=True)
    copy = pltpu.make_async_copy(asked, scalars, sem)
    copy.start()
    copy.wait()
    for d in range(devices):
        out[d] = table[jnp.clip(scalars[0, d], 0, owned - 1)]


def fetch(rows, table):
    devices = rows.shape[0]
    return pl.pallas_call(
        fetch_kernel,
        out_shape=[
            jax.ShapeDtypeStruct((devices,) + table.shape[1:], table.dtype),
            jax.ShapeDtypeStruct((1, devices), jnp.int32),
        ],
        in_specs=[VMEM, VMEM],
        out_specs=[VMEM, VMEM],
        scratch_shapes=[pltpu.SMEM((1, devices), jnp.int32), pltpu.SemaphoreType.DMA],
        compiler_params=pltpu.CompilerParams(vmem_limit_bytes=16 * MIB),
        name="fetch",
    )(rows, table)


def decode_kernel(
    owner,
    incoming,
    gain_query,
    gain_key,
    gain_out,
    w_query,
    w_key,
    w_value,
    w_out,
    out,
    attended_t,
    w_value_t,
):
    images = owner.shape[0] * owner.shape[1]
    width = incoming.shape[2]
    rows = STEP * TOK
    block = GROUP * TOK

    lane_image = lax.broadcasted_iota(jnp.int32, (TOK, block), 1) // TOK
    row_image = lax.broadcasted_iota(jnp.int32, (block, block), 0) // TOK
    column_image = lax.broadcasted_iota(jnp.int32, (block, block), 1) // TOK
    partner = ((row_image ^ 1) == column_image).astype(F32).astype(BF16)
    partner = jnp.concatenate([partner, partner], axis=1)
    lane_head = lax.broadcasted_iota(jnp.int32, (block, QUAD * HD), 1) // HD
    low_mask = [(lane_head % 2 == n).astype(F32).astype(BF16) for n in range(2)]
    high_mask = [(lane_head // 2 == n).astype(F32).astype(BF16) for n in range(2)]
    to_query = gain_query[...].reshape(1, width)
    to_key = gain_key[...].reshape(1, width)
    to_out = gain_out[...].reshape(1, width)

    for it in range(images // STEP):
        here = [owner[i % 2, i // 2] for i in range(it * STEP, (it + 1) * STEP)]
        x = jnp.stack([incoming[device] for device in here]).reshape(rows, width).astype(F32)
        xn = normalised(x)
        query_in = (xn * to_query).astype(BF16)
        context_in = (xn * to_key).astype(BF16)
        query = dot(query_in, w_query[...], ((1,), (0,))).astype(BF16)
        key = dot(context_in, w_key[...], ((1,), (0,))).astype(BF16)
        if it == 0:
            w_value_t[...] = w_value[...].T
        value_t = dot(w_value_t[...], context_in, ((1,), (1,))).astype(BF16)

        def score(g):
            at = slice(g * block, (g + 1) * block)
            compact = []
            for c in range(HEADS // QUAD):
                lanes = slice(c * QUAD * HD, (c + 1) * QUAD * HD)
                keys = [key[at, lanes] * low_mask[n] for n in range(2)]
                queries = [query[at, lanes] * high_mask[n] for n in range(2)]
                s_t = dot(
                    jnp.concatenate(keys, axis=0), jnp.concatenate(queries, axis=0), ((1,), (1,))
                ).reshape(2, GROUP, TOK, 2 * block)
                for h in range(QUAD):
                    part = slice(h // 2 * block, (h // 2 + 1) * block)
                    scores = s_t[h % 2, 1, :, part]
                    for i in range(1, GROUP):
                        scores = jnp.where(lane_image == i, s_t[h % 2, i ^ 1, :, part], scores)
                    compact.append(scores)
            return jnp.stack(compact) * (HD ** -0.5)

        def softmax(scores):
            e = jnp.exp(scores - jnp.max(scores, axis=1, keepdims=True))
            return (e / jnp.sum(e, axis=1, keepdims=True)).astype(BF16)

        def attend(g, weights):
            at = slice(g * block, (g + 1) * block)
            for head in range(0, HEADS, 2):
                two = jnp.concatenate([weights[head], weights[head + 1]], axis=1)
                p_t = jnp.concatenate([two] * GROUP, axis=0) * partner
                features = slice(head * HD, (head + 2) * HD)
                both = dot(value_t[features, at], p_t, ((1,), (0,))).astype(BF16)
                attended_t[head * HD:(head + 1) * HD, at] = both[:HD, :block]
                attended_t[(head + 1) * HD:(head + 2) * HD, at] = both[HD:, block:]

        groups = rows // block
        scores, weights = score(0), None
        for g in range(groups + 1):
            later = score(g + 1) if g + 1 < groups else None
            if weights is not None:
                attend(g - 1, weights)
            weights = softmax(scores) if scores is not None else None
            scores = later
        hidden = x + dot(attended_t[...], w_out[...], ((0,), (0,)))
        head_in = (normalised(hidden) * to_out).astype(BF16).reshape(STEP, TOK, width)
        for i in range(STEP):
            out[here[i]] = head_in[i]


def decode(owner, incoming, *parameters):
    images = owner.size
    devices, tokens, width = incoming.shape
    return pl.pallas_call(
        decode_kernel,
        out_shape=jax.ShapeDtypeStruct(incoming.shape, BF16),
        in_specs=[SMEM] + [VMEM] * 8,
        out_specs=VMEM,
        scratch_shapes=[
            pltpu.VMEM((width, STEP * tokens), BF16),
            pltpu.VMEM((width, width), BF16),
        ],
        compiler_params=pltpu.CompilerParams(vmem_limit_bytes=40 * MIB),
        name="decode",
    )(owner, incoming, *parameters)


def total_kernel(asked, returned, w_head, out, even, odd, result, sem):
    devices, tokens, width = returned.shape
    owned = out.shape[0]
    even[...] = jnp.zeros_like(even)
    odd[...] = jnp.zeros_like(odd)
    for d in range(devices):
        sums = odd if d % 2 else even
        image = jnp.where(asked[0, d] >= 0, asked[0, d], owned)
        sums[image] += returned[d].astype(F32)
    part = owned // sem.shape[0]
    copies = []
    for n in range(sem.shape[0]):
        at = slice(n * part, (n + 1) * part)
        whole = (even[at] + odd[at]).reshape(part * tokens, width).astype(BF16)
        head = dot(whole, w_head[...], ((1,), (0,))).astype(BF16)
        result[at] = head.reshape(part, tokens, w_head.shape[1])
        copies.append(pltpu.make_async_copy(result.at[at], out.at[at], sem.at[n]))
        copies[-1].start()
    for copy in copies:
        copy.wait()


def total(asked, returned, w_head, owned):
    devices, tokens, width = returned.shape
    shape = (owned, tokens, w_head.shape[1])
    return pl.pallas_call(
        total_kernel,
        out_shape=jax.ShapeDtypeStruct(shape, BF16),
        in_specs=[SMEM, VMEM, VMEM],
        out_specs=HBM,
        scratch_shapes=[
            pltpu.VMEM((owned + 1, tokens, width), F32),
            pltpu.VMEM((owned + 1, tokens, width), F32),
            pltpu.VMEM(shape, BF16),
            pltpu.SemaphoreType.DMA((2,)),
        ],
        compiler_params=pltpu.CompilerParams(vmem_limit_bytes=24 * MIB),
        name="total",
    )(asked, returned, w_head)


def on_device(
    encoder_tokens,
    pair_owner,
    pair_local,
    w_embed,
    gain_query,
    gain_key,
    gain_out,
    w_query,
    w_key,
    w_value,
    w_out,
    w_head,
):
    devices = lax.axis_size(AXES)
    owned, tokens, _ = encoder_tokens.shape
    owner = pair_owner.T
    rows = exchange(ask(owner, pair_local.T, devices))
    table = jnp.dot(
        encoder_tokens.reshape(owned * tokens, -1), w_embed, preferred_element_type=F32
    ).astype(BF16).reshape(owned, tokens, -1)
    outgoing, asked = fetch(rows, table)
    incoming = exchange(outgoing)
    going_back = decode(
        owner, incoming, gain_query, gain_key, gain_out, w_query, w_key, w_value, w_out
    )
    return total(asked, exchange(going_back), w_head, owned)


def solution(mesh):
    spec = P(AXES)
    return jax.shard_map(
        on_device,
        mesh=mesh,
        in_specs=(spec,) * 3 + (P(),) * 9,
        out_specs=spec,
        check_vma=False,
    )
```

```python
import jax
import jax.numpy as jnp
from jax import lax
from jax.experimental import pallas as pl
from jax.experimental.pallas import tpu as pltpu
from jax.sharding import PartitionSpec as P

HEADS = 12
HD = 64
TOK = 16
AXES = ("img", "pair")
GROUP = 8
QUAD = 4
STEP = 32
BF16 = jnp.bfloat16
F32 = jnp.float32
MIB = 1024 * 1024
VMEM = pl.BlockSpec(memory_space=pltpu.VMEM)
SMEM = pl.BlockSpec(memory_space=pltpu.SMEM)
HBM = pl.BlockSpec(memory_space=pltpu.HBM)


def exchange(blocks):
    return lax.all_to_all(blocks, AXES, split_axis=0, concat_axis=0, tiled=True)


def dot(a, b, contract):
    return lax.dot_general(a, b, (contract, ((), ())), preferred_element_type=F32)


def normalised(values):
    mean = jnp.mean(values, axis=-1, keepdims=True)
    centred = values - mean
    spread = jnp.mean(centred * centred, axis=-1, keepdims=True)
    return centred * lax.rsqrt(spread + 1e-05)


def ask_kernel(owner_hbm, local_hbm, out, owner, local, sem):
    devices = out.shape[0]
    sides, slots = owner.shape
    copies = [
        pltpu.make_async_copy(owner_hbm, owner, sem.at[0]),
        pltpu.make_async_copy(local_hbm, local, sem.at[1]),
    ]
    for copy in copies:
        copy.start()
    for copy in copies:
        copy.wait()
    device = lax.broadcasted_iota(jnp.int32, (devices, slots), 0)
    found = jnp.zeros((devices, slots), jnp.int32)
    for side in range(sides):
        match = device == owner[side:side + 1, :]
        found = jnp.where(match, local[side:side + 1, :] + 1, found)
    wanted = jnp.sum(found, axis=1, keepdims=True) - 1
    out[...] = jnp.broadcast_to(wanted, out.shape)


def ask(owner, local, devices):
    return pl.pallas_call(
        ask_kernel,
        out_shape=jax.ShapeDtypeStruct((devices, devices), jnp.int32),
        in_specs=[HBM, HBM],
        out_specs=VMEM,
        scratch_shapes=[
            pltpu.VMEM(owner.shape, jnp.int32),
            pltpu.VMEM(owner.shape, jnp.int32),
            pltpu.SemaphoreType.DMA((2,)),
        ],
        compiler_params=pltpu.CompilerParams(vmem_limit_bytes=62 * MIB),
        name="ask",
    )(owner, local)


def fetch_kernel(rows, table, out, asked, scalars, sem):
    devices = out.shape[0]
    owned = table.shape[0]
    square = rows.shape
    across = lax.broadcasted_iota(jnp.int32, square, 0) == lax.broadcasted_iota(jnp.int32, square, 1)
    asked[...] = jnp.sum(jnp.where(across, rows[...], 0), axis=0, keepdims=True)
    copy = pltpu.make_async_copy(asked, scalars, sem)
    copy.start()
    copy.wait()
    for d in range(devices):
        out[d] = table[jnp.clip(scalars[0, d], 0, owned - 1)]


def fetch(rows, table):
    devices = rows.shape[0]
    return pl.pallas_call(
        fetch_kernel,
        out_shape=[
            jax.ShapeDtypeStruct((devices,) + table.shape[1:], table.dtype),
            jax.ShapeDtypeStruct((1, devices), jnp.int32),
        ],
        in_specs=[VMEM, VMEM],
        out_specs=[VMEM, VMEM],
        scratch_shapes=[pltpu.SMEM((1, devices), jnp.int32), pltpu.SemaphoreType.DMA],
        compiler_params=pltpu.CompilerParams(vmem_limit_bytes=16 * MIB),
        name="fetch",
    )(rows, table)


def decode_kernel(
    owner,
    incoming,
    gain_query,
    gain_key,
    gain_out,
    w_query,
    w_key,
    w_value,
    w_out,
    out,
    attended_t,
    w_value_t,
):
    images = owner.shape[0] * owner.shape[1]
    width = incoming.shape[2]
    rows = STEP * TOK
    block = GROUP * TOK

    lane_image = lax.broadcasted_iota(jnp.int32, (TOK, block), 1) // TOK
    row_image = lax.broadcasted_iota(jnp.int32, (block, block), 0) // TOK
    column_image = lax.broadcasted_iota(jnp.int32, (block, block), 1) // TOK
    partner = ((row_image ^ 1) == column_image).astype(F32).astype(BF16)
    partner = jnp.concatenate([partner, partner], axis=1)
    lane_head = lax.broadcasted_iota(jnp.int32, (block, QUAD * HD), 1) // HD
    low_mask = [(lane_head % 2 == n).astype(F32).astype(BF16) for n in range(2)]
    high_mask = [(lane_head // 2 == n).astype(F32).astype(BF16) for n in range(2)]
    to_query = gain_query[...].reshape(1, width)
    to_key = gain_key[...].reshape(1, width)
    to_out = gain_out[...].reshape(1, width)

    for it in range(images // STEP):
        here = [owner[i % 2, i // 2] for i in range(it * STEP, (it + 1) * STEP)]
        x = jnp.stack([incoming[device] for device in here]).reshape(rows, width).astype(F32)
        xn = normalised(x)
        query_in = (xn * to_query).astype(BF16)
        context_in = (xn * to_key).astype(BF16)
        query = dot(query_in, w_query[...], ((1,), (0,))).astype(BF16)
        key = dot(context_in, w_key[...], ((1,), (0,))).astype(BF16)
        if it == 0:
            w_value_t[...] = w_value[...].T
        value_t = dot(w_value_t[...], context_in, ((1,), (1,))).astype(BF16)

        def score(g):
            at = slice(g * block, (g + 1) * block)
            compact = []
            for c in range(HEADS // QUAD):
                lanes = slice(c * QUAD * HD, (c + 1) * QUAD * HD)
                keys = [key[at, lanes] * low_mask[n] for n in range(2)]
                queries = [query[at, lanes] * high_mask[n] for n in range(2)]
                s_t = dot(
                    jnp.concatenate(keys, axis=0), jnp.concatenate(queries, axis=0), ((1,), (1,))
                ).reshape(2, GROUP, TOK, 2 * block)
                for h in range(QUAD):
                    part = slice(h // 2 * block, (h // 2 + 1) * block)
                    scores = s_t[h % 2, 1, :, part]
                    for i in range(1, GROUP):
                        scores = jnp.where(lane_image == i, s_t[h % 2, i ^ 1, :, part], scores)
                    compact.append(scores)
            return jnp.stack(compact) * (HD ** -0.5)

        def softmax(scores):
            e = jnp.exp(scores - jnp.max(scores, axis=1, keepdims=True))
            return (e / jnp.sum(e, axis=1, keepdims=True)).astype(BF16)

        def attend(g, weights):
            at = slice(g * block, (g + 1) * block)
            for head in range(0, HEADS, 2):
                two = jnp.concatenate([weights[head], weights[head + 1]], axis=1)
                p_t = jnp.concatenate([two] * GROUP, axis=0) * partner
                features = slice(head * HD, (head + 2) * HD)
                both = dot(value_t[features, at], p_t, ((1,), (0,))).astype(BF16)
                attended_t[head * HD:(head + 1) * HD, at] = both[:HD, :block]
                attended_t[(head + 1) * HD:(head + 2) * HD, at] = both[HD:, block:]

        groups = rows // block
        scores, weights = score(0), None
        for g in range(groups + 1):
            later = score(g + 1) if g + 1 < groups else None
            if weights is not None:
                attend(g - 1, weights)
            weights = softmax(scores) if scores is not None else None
            scores = later
        hidden = jnp.concatenate(
            [
                x[n:n + 2 * block] + dot(attended_t[:, n:n + 2 * block], w_out[...], ((0,), (0,)))
                for n in range(0, rows, 2 * block)
            ],
            axis=0,
        )
        head_in = (normalised(hidden) * to_out).astype(BF16).reshape(STEP, TOK, width)
        for i in range(STEP):
            out[here[i]] = head_in[i]


def decode(owner, incoming, *parameters):
    images = owner.size
    devices, tokens, width = incoming.shape
    return pl.pallas_call(
        decode_kernel,
        out_shape=jax.ShapeDtypeStruct(incoming.shape, BF16),
        in_specs=[SMEM] + [VMEM] * 8,
        out_specs=VMEM,
        scratch_shapes=[
            pltpu.VMEM((width, STEP * tokens), BF16),
            pltpu.VMEM((width, width), BF16),
        ],
        compiler_params=pltpu.CompilerParams(vmem_limit_bytes=40 * MIB),
        name="decode",
    )(owner, incoming, *parameters)


def total_kernel(asked_vmem, returned, w_head, out, even, odd, result, asked, sem, asked_sem):
    devices, tokens, width = returned.shape
    owned = out.shape[0]
    copy = pltpu.make_async_copy(asked_vmem, asked, asked_sem)
    copy.start()
    even[...] = jnp.zeros_like(even)
    odd[...] = jnp.zeros_like(odd)
    copy.wait()
    for d in range(devices):
        sums = odd if d % 2 else even
        image = jnp.where(asked[0, d] >= 0, asked[0, d], owned)
        sums[image] += returned[d].astype(F32)
    copies = []
    cuts = (0, owned // 2, 3 * owned // 4, owned)
    for n in range(sem.shape[0]):
        at = slice(cuts[n], cuts[n + 1])
        part = cuts[n + 1] - cuts[n]
        whole = (even[at] + odd[at]).reshape(part * tokens, width).astype(BF16)
        head = dot(whole, w_head[...], ((1,), (0,))).astype(BF16)
        result[at] = head.reshape(part, tokens, w_head.shape[1])
        copies.append(pltpu.make_async_copy(result.at[at], out.at[at], sem.at[n]))
        copies[-1].start()
    for copy in copies:
        copy.wait()


def total(asked, returned, w_head, owned):
    devices, tokens, width = returned.shape
    shape = (owned, tokens, w_head.shape[1])
    return pl.pallas_call(
        total_kernel,
        out_shape=jax.ShapeDtypeStruct(shape, BF16),
        in_specs=[VMEM, VMEM, VMEM],
        out_specs=HBM,
        scratch_shapes=[
            pltpu.VMEM((owned + 1, tokens, width), F32),
            pltpu.VMEM((owned + 1, tokens, width), F32),
            pltpu.VMEM(shape, BF16),
            pltpu.SMEM(asked.shape, jnp.int32),
            pltpu.SemaphoreType.DMA((3,)),
            pltpu.SemaphoreType.DMA,
        ],
        compiler_params=pltpu.CompilerParams(vmem_limit_bytes=24 * MIB),
        name="total",
    )(asked, returned, w_head)


def on_device(
    encoder_tokens,
    pair_owner,
    pair_local,
    w_embed,
    gain_query,
    gain_key,
    gain_out,
    w_query,
    w_key,
    w_value,
    w_out,
    w_head,
):
    devices = lax.axis_size(AXES)
    owned, tokens, _ = encoder_tokens.shape
    owner = pair_owner.T
    rows = exchange(ask(owner, pair_local.T, devices))
    table = jnp.dot(
        encoder_tokens.reshape(owned * tokens, -1), w_embed, preferred_element_type=F32
    ).astype(BF16).reshape(owned, tokens, -1)
    outgoing, asked = fetch(rows, table)
    incoming = exchange(outgoing)
    going_back = decode(
        owner, incoming, gain_query, gain_key, gain_out, w_query, w_key, w_value, w_out
    )
    return total(asked, exchange(going_back), w_head, owned)


def solution(mesh):
    spec = P(AXES)
    return jax.shard_map(
        on_device,
        mesh=mesh,
        in_specs=(spec,) * 3 + (P(),) * 9,
        out_specs=spec,
        check_vma=False,
    )
```

```python
import jax
import jax.numpy as jnp
from jax import lax
from jax.experimental import pallas as pl
from jax.experimental.pallas import tpu as pltpu
from jax.sharding import PartitionSpec as P

HEADS = 12
HD = 64
TOK = 16
AXES = ("img", "pair")
GROUP = 8
QUAD = 4
STEP = 32
BF16 = jnp.bfloat16
F32 = jnp.float32
MIB = 1024 * 1024
VMEM = pl.BlockSpec(memory_space=pltpu.VMEM)
SMEM = pl.BlockSpec(memory_space=pltpu.SMEM)
HBM = pl.BlockSpec(memory_space=pltpu.HBM)


def exchange(blocks):
    return lax.all_to_all(blocks, AXES, split_axis=0, concat_axis=0, tiled=True)


def dot(a, b, contract):
    return lax.dot_general(a, b, (contract, ((), ())), preferred_element_type=F32)


def normalised(values):
    mean = jnp.mean(values, axis=-1, keepdims=True)
    centred = values - mean
    spread = jnp.mean(centred * centred, axis=-1, keepdims=True)
    return centred * lax.rsqrt(spread + 1e-05)


def ask_kernel(owner_hbm, local_hbm, out, owner, local, sem):
    devices = out.shape[0]
    sides, slots = owner.shape
    copies = [
        pltpu.make_async_copy(owner_hbm, owner, sem.at[0]),
        pltpu.make_async_copy(local_hbm, local, sem.at[1]),
    ]
    for copy in copies:
        copy.start()
    for copy in copies:
        copy.wait()
    device = lax.broadcasted_iota(jnp.int32, (devices, slots), 0)
    found = jnp.zeros((devices, slots), jnp.int32)
    for side in range(sides):
        match = device == owner[side:side + 1, :]
        found = jnp.where(match, local[side:side + 1, :] + 1, found)
    wanted = jnp.sum(found, axis=1, keepdims=True) - 1
    out[...] = jnp.broadcast_to(wanted, out.shape)


def ask(owner, local, devices):
    return pl.pallas_call(
        ask_kernel,
        out_shape=jax.ShapeDtypeStruct((devices, devices), jnp.int32),
        in_specs=[HBM, HBM],
        out_specs=VMEM,
        scratch_shapes=[
            pltpu.VMEM(owner.shape, jnp.int32),
            pltpu.VMEM(owner.shape, jnp.int32),
            pltpu.SemaphoreType.DMA((2,)),
        ],
        compiler_params=pltpu.CompilerParams(vmem_limit_bytes=62 * MIB),
        name="ask",
    )(owner, local)


def fetch_kernel(rows, table, out, asked, scalars, sem):
    devices = out.shape[0]
    owned = table.shape[0]
    square = rows.shape
    across = lax.broadcasted_iota(jnp.int32, square, 0) == lax.broadcasted_iota(jnp.int32, square, 1)
    asked[...] = jnp.sum(jnp.where(across, rows[...], 0), axis=0, keepdims=True)
    copy = pltpu.make_async_copy(asked, scalars, sem)
    copy.start()
    copy.wait()
    for d in range(devices):
        out[d] = table[jnp.clip(scalars[0, d], 0, owned - 1)]


def fetch(rows, table):
    devices = rows.shape[0]
    return pl.pallas_call(
        fetch_kernel,
        out_shape=[
            jax.ShapeDtypeStruct((devices,) + table.shape[1:], table.dtype),
            jax.ShapeDtypeStruct((1, devices), jnp.int32),
        ],
        in_specs=[VMEM, VMEM],
        out_specs=[VMEM, VMEM],
        scratch_shapes=[pltpu.SMEM((1, devices), jnp.int32), pltpu.SemaphoreType.DMA],
        compiler_params=pltpu.CompilerParams(vmem_limit_bytes=16 * MIB),
        name="fetch",
    )(rows, table)


def decode_kernel(
    owner,
    incoming,
    gain_query,
    gain_key,
    gain_out,
    w_query,
    w_key,
    w_value,
    w_out,
    out,
    attended_t,
    w_value_t,
):
    images = owner.shape[0] * owner.shape[1]
    width = incoming.shape[2]
    rows = STEP * TOK
    block = GROUP * TOK

    lane_image = lax.broadcasted_iota(jnp.int32, (TOK, block), 1) // TOK
    row_image = lax.broadcasted_iota(jnp.int32, (block, block), 0) // TOK
    column_image = lax.broadcasted_iota(jnp.int32, (block, block), 1) // TOK
    partner = ((row_image ^ 1) == column_image).astype(F32).astype(BF16)
    partner = jnp.concatenate([partner, partner], axis=1)
    lane_head = lax.broadcasted_iota(jnp.int32, (block, QUAD * HD), 1) // HD
    low_mask = [(lane_head % 2 == n).astype(F32).astype(BF16) for n in range(2)]
    high_mask = [(lane_head // 2 == n).astype(F32).astype(BF16) for n in range(2)]
    to_query = gain_query[...].reshape(1, width)
    to_key = gain_key[...].reshape(1, width)
    to_out = gain_out[...].reshape(1, width)

    for it in range(images // STEP):
        here = [owner[i % 2, i // 2] for i in range(it * STEP, (it + 1) * STEP)]
        x = jnp.stack([incoming[device] for device in here]).reshape(rows, width).astype(F32)
        xn = normalised(x)
        query_in = (xn * to_query).astype(BF16)
        context_in = (xn * to_key).astype(BF16)
        pieces = [slice(n, n + 2 * block) for n in range(0, rows, 2 * block)]
        query, key = (
            jnp.concatenate([dot(a[n], w[...], ((1,), (0,))).astype(BF16) for n in pieces], axis=0)
            for a, w in ((query_in, w_query), (context_in, w_key))
        )
        if it == 0:
            w_value_t[...] = w_value[...].T
        value_t = dot(w_value_t[...], context_in, ((1,), (1,))).astype(BF16)

        def score(g):
            at = slice(g * block, (g + 1) * block)
            compact = []
            for c in range(HEADS // QUAD):
                lanes = slice(c * QUAD * HD, (c + 1) * QUAD * HD)
                keys = [key[at, lanes] * low_mask[n] for n in range(2)]
                queries = [query[at, lanes] * high_mask[n] for n in range(2)]
                s_t = dot(
                    jnp.concatenate(keys, axis=0), jnp.concatenate(queries, axis=0), ((1,), (1,))
                ).reshape(2, GROUP, TOK, 2 * block)
                for h in range(QUAD):
                    part = slice(h // 2 * block, (h // 2 + 1) * block)
                    scores = s_t[h % 2, 1, :, part]
                    for i in range(1, GROUP):
                        scores = jnp.where(lane_image == i, s_t[h % 2, i ^ 1, :, part], scores)
                    compact.append(scores)
            return jnp.stack(compact) * (HD ** -0.5)

        def softmax(scores):
            e = jnp.exp(scores - jnp.max(scores, axis=1, keepdims=True))
            return (e / jnp.sum(e, axis=1, keepdims=True)).astype(BF16)

        def attend(g, weights):
            at = slice(g * block, (g + 1) * block)
            for head in range(0, HEADS, 2):
                two = jnp.concatenate([weights[head], weights[head + 1]], axis=1)
                p_t = jnp.concatenate([two] * GROUP, axis=0) * partner
                features = slice(head * HD, (head + 2) * HD)
                both = dot(value_t[features, at], p_t, ((1,), (0,))).astype(BF16)
                attended_t[head * HD:(head + 1) * HD, at] = both[:HD, :block]
                attended_t[(head + 1) * HD:(head + 2) * HD, at] = both[HD:, block:]

        groups = rows // block
        scores, weights = score(0), None
        for g in range(groups + 1):
            later = score(g + 1) if g + 1 < groups else None
            if weights is not None:
                attend(g - 1, weights)
            weights = softmax(scores) if scores is not None else None
            scores = later
        hidden = jnp.concatenate(
            [
                x[n:n + 2 * block] + dot(attended_t[:, n:n + 2 * block], w_out[...], ((0,), (0,)))
                for n in range(0, rows, 2 * block)
            ],
            axis=0,
        )
        head_in = (normalised(hidden) * to_out).astype(BF16).reshape(STEP, TOK, width)
        for i in range(STEP):
            out[here[i]] = head_in[i]


def decode(owner, incoming, *parameters):
    images = owner.size
    devices, tokens, width = incoming.shape
    return pl.pallas_call(
        decode_kernel,
        out_shape=jax.ShapeDtypeStruct(incoming.shape, BF16),
        in_specs=[SMEM] + [VMEM] * 8,
        out_specs=VMEM,
        scratch_shapes=[
            pltpu.VMEM((width, STEP * tokens), BF16),
            pltpu.VMEM((width, width), BF16),
        ],
        compiler_params=pltpu.CompilerParams(vmem_limit_bytes=40 * MIB),
        name="decode",
    )(owner, incoming, *parameters)


def total_kernel(asked_vmem, returned, w_head, out, even, odd, result, asked, sem, asked_sem):
    devices, tokens, width = returned.shape
    owned = out.shape[0]
    copy = pltpu.make_async_copy(asked_vmem, asked, asked_sem)
    copy.start()
    even[...] = jnp.zeros_like(even)
    odd[...] = jnp.zeros_like(odd)
    copy.wait()
    for d in range(devices):
        sums = odd if d % 2 else even
        image = jnp.where(asked[0, d] >= 0, asked[0, d], owned)
        sums[image] += returned[d].astype(F32)
    copies = []
    cuts = (0, owned // 2, 3 * owned // 4, owned)
    for n in range(sem.shape[0]):
        at = slice(cuts[n], cuts[n + 1])
        part = cuts[n + 1] - cuts[n]
        whole = (even[at] + odd[at]).reshape(part * tokens, width).astype(BF16)
        head = dot(whole, w_head[...], ((1,), (0,))).astype(BF16)
        result[at] = head.reshape(part, tokens, w_head.shape[1])
        copies.append(pltpu.make_async_copy(result.at[at], out.at[at], sem.at[n]))
        copies[-1].start()
    for copy in copies:
        copy.wait()


def total(asked, returned, w_head, owned):
    devices, tokens, width = returned.shape
    shape = (owned, tokens, w_head.shape[1])
    return pl.pallas_call(
        total_kernel,
        out_shape=jax.ShapeDtypeStruct(shape, BF16),
        in_specs=[VMEM, VMEM, VMEM],
        out_specs=HBM,
        scratch_shapes=[
            pltpu.VMEM((owned + 1, tokens, width), F32),
            pltpu.VMEM((owned + 1, tokens, width), F32),
            pltpu.VMEM(shape, BF16),
            pltpu.SMEM(asked.shape, jnp.int32),
            pltpu.SemaphoreType.DMA((3,)),
            pltpu.SemaphoreType.DMA,
        ],
        compiler_params=pltpu.CompilerParams(vmem_limit_bytes=24 * MIB),
        name="total",
    )(asked, returned, w_head)


def on_device(
    encoder_tokens,
    pair_owner,
    pair_local,
    w_embed,
    gain_query,
    gain_key,
    gain_out,
    w_query,
    w_key,
    w_value,
    w_out,
    w_head,
):
    devices = lax.axis_size(AXES)
    owned, tokens, _ = encoder_tokens.shape
    owner = pair_owner.T
    rows = exchange(ask(owner, pair_local.T, devices))
    table = jnp.dot(
        encoder_tokens.reshape(owned * tokens, -1), w_embed, preferred_element_type=F32
    ).astype(BF16).reshape(owned, tokens, -1)
    outgoing, asked = fetch(rows, table)
    incoming = exchange(outgoing)
    going_back = decode(
        owner, incoming, gain_query, gain_key, gain_out, w_query, w_key, w_value, w_out
    )
    return total(asked, exchange(going_back), w_head, owned)


def solution(mesh):
    spec = P(AXES)
    return jax.shard_map(
        on_device,
        mesh=mesh,
        in_specs=(spec,) * 3 + (P(),) * 9,
        out_specs=spec,
        check_vma=False,
    )
```
